32 devices in a mesh: groups: 2 (over x), seq: 8 (over z, y), tp: 2 (over core).
Axes of the slice: x: 2, y: 2, z: 4, core: 2. Of those that a mesh axis runs over, the one named last changes fastest.
Arguments:
- token_ids: int32 [2048], P(('groups', 'seq')), parts along dimension 0, may hold values from 0 to 511
- embed_table: bfloat16 [512, 4096], P(None, 'tp'), may hold values from -4 to 4
- hyena_qkv: bfloat16 [3, 2048, 4096], P(None, ('groups', 'seq'), 'tp'), parts along dimension 1, may hold values from -5 to 5
- conv_weights: float32 [3, 3, 4096], P(None, None, 'tp'), may hold values from -2.5 to 2.5
- decay_rates: float32 [8, 4096], P(None, 'tp'), may hold values from 0 to 1, as said below
- residues: float32 [8, 4096], P(None, 'tp'), may hold values from -2 to 2
- prior_state: float32 [16, 4096], P('groups', 'tp'), parts along dimension 0, may hold values from -4 to 4
Outputs:
- hyena_out: bfloat16 [2048, 4096], P(('groups', 'seq'), 'tp'), parts along dimension 0
- end_state: float32 [16, 4096], P('groups', ('tp', 'seq')), parts along dimension 0
The draws below stay inside these ranges and needn't reach their ends.
There are 2 independent parts, one for each index of `groups`. The reference program is written for one: setup_inputs(seed, part) draws one part's arguments, and reference() takes and returns one part's arrays. A program takes and returns all parts, laid end to end along the dimension named above; an argument that names none is the same for every part. Nothing has to cross between parts.
Inputs may be any that keep to these rules, and one draw needn't show every extreme that they name: `decay_rates`: decay rates of the modes, positive.
All inputs are finite; a program needn't handle non-finite values.
Results may differ from the reference program's by a relative error of at most 0.001.
Values may be sent and summed in bfloat16 or wider, within the bound.
A program may use at most 128 MiB of HBM per device.

```python
import math
import jax
import jax.numpy as jnp
from jax import lax

D = 4096
VOCAB = 512
ORDER = 8
SHORT = 3
TOK_DEV = 128
TOKENS = 1024


def spread_rates(key, shape, low_end, high_end):
    return jnp.exp(jax.random.uniform(key, shape, jnp.float32, math.log(low_end), math.log(high_end)))


def draw_decay_rates(key, part):
    key_c, key_s, key_l, key_h, key_f = jax.random.split(jax.random.fold_in(key, 11), 5)
    shape = (ORDER, D)
    chooser = jax.random.uniform(key_c, shape, jnp.float32)
    first_cut = 0.3
    second_cut = 0.5
    third_cut = 0.75
    slow_rate = spread_rates(key_s, shape, 0.05 / TOKENS, 2.0 / TOKENS)
    lower_rate = spread_rates(key_l, shape, 0.3 / TOK_DEV, 0.95 / TOK_DEV)
    upper_rate = spread_rates(key_h, shape, 1.05 / TOK_DEV, 1.6 / TOK_DEV)
    fast_rate = spread_rates(key_f, shape, 1.0 / 48.0, 1.0 / 24.0)
    middle_rate = jnp.where(chooser < second_cut, lower_rate, jnp.where(chooser < third_cut, upper_rate, fast_rate))
    return jnp.where(chooser < first_cut, slow_rate, middle_rate).astype(jnp.float32)


def set_ends(drawn, key, low, top_value):
    longest = drawn.shape.index(max(drawn.shape))
    spots = []
    for shift in (0, 1):
        where = [jax.random.randint(jax.random.fold_in(key, axis), (), 0, length) for axis, length in enumerate(drawn.shape)]
        where[longest] = (where[longest] + shift) % drawn.shape[longest]
        spots.append(tuple(where))
    return drawn.at[spots[0]].set(low).at[spots[1]].set(top_value)


def levels(key, shape, shards, least, high):
    loudness, own = 1.0, jax.random.fold_in(key, 6)
    for position, shards_of in shards:
        draws = jnp.exp(jax.random.uniform(jax.random.fold_in(own, position), (shards_of,), jnp.float32, least / len(shards), high / len(shards)))
        loudness = loudness * jnp.repeat(draws, shape[position] // shards_of).reshape([-1 if axis == position else 1 for axis in range(len(shape))])
    return loudness


def scatter_about(rng, extent, width, bound, cuts=(), dtype=jnp.bfloat16):
    level = levels(rng, extent, cuts, -0.22, 0.18) if cuts else 1.0
    drawn = jax.random.normal(rng, extent, jnp.float32) * width * level
    return jnp.minimum(jnp.maximum(drawn, -bound), bound).astype(dtype)


def setup_inputs(seed: int = 0, part: int = 0) -> dict:
    streams_of = jax.random.split(jax.random.key(seed), 8)
    part_splits = jax.random.split(jax.random.fold_in(streams_of[7], part), 8)
    token_ids = set_ends(jax.random.randint(part_splits[0], (TOKENS,), 0, VOCAB), jax.random.fold_in(part_splits[0], 1), 0, VOCAB - 1).astype(jnp.int32)
    embed_table = scatter_about(streams_of[1], (VOCAB, D), 1.0, 4.0, ((1, 2),))
    hyena_qkv = scatter_about(part_splits[2], (3, TOKENS, D), 1.0, 5.0, ((1, 8), (2, 2)))
    conv_weights = scatter_about(streams_of[3], (3, SHORT, D), 0.6, 2.5, ((2, 2),), jnp.float32)
    decay_rates = draw_decay_rates(jax.random.fold_in(streams_of[7], 71), part)
    residues = scatter_about(streams_of[5], (ORDER, D), ORDER ** -0.5, 2.0, ((1, 2),), jnp.float32)
    prior_state = scatter_about(part_splits[6], (ORDER, D), 1.0, 4.0, ((1, 2),), jnp.float32)
    return dict(token_ids=token_ids, embed_table=embed_table, hyena_qkv=hyena_qkv, conv_weights=conv_weights, decay_rates=decay_rates, residues=residues, prior_state=prior_state)


def short_conv(signal, tap_weights):
    tok_count = signal.shape[0]
    widened = signal.astype(jnp.float32)
    total = jnp.zeros(widened.shape, jnp.float32)
    for tap_index in range(tap_weights.shape[0]):
        shifted = jnp.pad(widened, ((tap_index, 0), (0, 0)))[:tok_count]
        total = total + tap_weights[tap_index][None, :] * shifted
    return total

def reference(token_ids, embed_table, hyena_qkv, conv_weights, decay_rates, residues, prior_state):
    q_feat = short_conv(hyena_qkv[0], conv_weights[0])
    k_feat = short_conv(hyena_qkv[1], conv_weights[1])
    v_feat = short_conv(hyena_qkv[2], conv_weights[2])
    product_in = k_feat * v_feat
    pole = jnp.exp(-decay_rates)
    gain = jnp.sqrt(-jnp.expm1(-2.0 * decay_rates))

    def advance(state, row):
        state = pole * state + gain * row[None, :]
        return (state, lax.optimization_barrier(jnp.sum(residues * state, axis=0)))
    end_state, filtered = lax.scan(advance, prior_state, product_in)
    embedded = embed_table[token_ids].astype(jnp.float32)
    hyena_out = (embedded + q_feat * filtered).astype(jnp.bfloat16)
    return (hyena_out, end_state)
```

```python
import functools
import jax
import jax.numpy as jnp
from jax import lax
from jax.experimental import pallas as pl
from jax.experimental.pallas import tpu as pltpu
from jax.sharding import PartitionSpec as P


def shifted(array, axis, by):
    size = lax.axis_size(axis)
    pairs = [(i, i + by) for i in range(size) if 0 <= i + by < size]
    return lax.ppermute(array, axis, pairs)


def short_features(extended, conv_weights, tok_local):
    tap_count = conv_weights.shape[1]
    results = []
    for member in range(3):
        total = jnp.zeros((tok_local, extended.shape[2]), jnp.float32)
        for tap_index in range(tap_count):
            offset = tap_count - 1 - tap_index
            total = total + conv_weights[member, tap_index][None, :] * extended[
                member, offset : offset + tok_local
            ].astype(jnp.float32)
        results.append(total)
    return results


def modal_local(product_in, decay_rates, residues, sub_len):
    tok_local, channels = product_in.shape
    block_count = tok_local // sub_len
    blocks = product_in.reshape(block_count, sub_len, channels)
    spacing = jnp.arange(sub_len, dtype=jnp.float32)
    gain = jnp.sqrt(-jnp.expm1(-2.0 * decay_rates))
    decay_table = jnp.exp(-decay_rates[:, None, :] * spacing[None, :, None])
    kernel = jnp.sum((residues * gain)[:, None, :] * decay_table, axis=0)
    extended = jnp.concatenate(
        [kernel[::-1], jnp.zeros((sub_len - 1, channels), jnp.float32)], axis=0
    )
    toeplitz = jnp.stack(
        [extended[sub_len - 1 - row : 2 * sub_len - 1 - row] for row in range(sub_len)], axis=0
    )
    inner = jnp.einsum("tsc,bsc->btc", toeplitz, blocks, precision=lax.Precision.HIGHEST)
    tail_weight = gain[:, None, :] * jnp.exp(
        -decay_rates[:, None, :] * (sub_len - 1 - spacing)[None, :, None]
    )
    closing = jnp.einsum("bsc,msc->bmc", blocks, tail_weight, precision=lax.Precision.HIGHEST)
    per_block = jnp.exp(-decay_rates * sub_len)

    def advance(carry, piece):
        return (per_block * carry + piece, carry)

    local_end, starts = lax.scan(advance, jnp.zeros_like(decay_rates), closing)
    return (inner, starts, local_end)


def modal_readout(inner, starts, incoming, decay_rates, residues, sub_len):
    block_count = starts.shape[0]
    block_pos = jnp.arange(block_count, dtype=jnp.float32) * sub_len
    opening = (
        starts + jnp.exp(-decay_rates[None, :, :] * block_pos[:, None, None]) * incoming[None, :, :]
    )
    spacing = jnp.arange(sub_len, dtype=jnp.float32)
    readout = residues[:, None, :] * jnp.exp(
        -decay_rates[:, None, :] * (spacing + 1.0)[None, :, None]
    )
    outer = jnp.einsum("bmc,mtc->btc", opening, readout, precision=lax.Precision.HIGHEST)
    return (inner + outer).reshape(block_count * sub_len, inner.shape[2])


def plain_body(token_ids, embed_table, hyena_qkv, conv_weights, decay_rates, residues, prior_state):
    tok_local = hyena_qkv.shape[1]
    tap_count = conv_weights.shape[1]
    seq_count = lax.axis_size("seq")
    seq_index = lax.axis_index("seq")
    tails_local = hyena_qkv[:, tok_local - (tap_count - 1) :, :]
    tails_prev = shifted(tails_local, "seq", 1)
    extended = jnp.concatenate([tails_prev, hyena_qkv], axis=1)
    q_feat, k_feat, v_feat = short_features(extended, conv_weights, tok_local)
    product_in = k_feat * v_feat
    sub_len = 16
    inner, starts, local_end = modal_local(product_in, decay_rates, residues, sub_len)
    piece = lax.all_gather(local_end[None], "seq", axis=0, tiled=True)
    count = piece.shape[0]
    sources = jnp.arange(count, dtype=jnp.int32)
    gap_len = jnp.maximum(seq_index - 1 - sources, 0).astype(jnp.float32) * tok_local
    factors = jnp.where(
        (sources < seq_index)[:, None, None],
        jnp.exp(-decay_rates[None, :, :] * gap_len[:, None, None]),
        0.0,
    )
    folded = jnp.sum(factors * piece, axis=0)
    incoming = (
        folded + jnp.exp(-decay_rates * (seq_index.astype(jnp.float32) * tok_local)) * prior_state
    )
    filtered = modal_readout(inner, starts, incoming, decay_rates, residues, sub_len)
    vocab_ids = jnp.arange(embed_table.shape[0], dtype=jnp.int32)
    one_hot = (token_ids[:, None] == vocab_ids[None, :]).astype(jnp.bfloat16)
    embedded = jnp.dot(one_hot, embed_table, preferred_element_type=jnp.float32)
    hyena_out = (embedded + q_feat * filtered).astype(jnp.bfloat16)
    lag_after = (seq_count - 1 - seq_index).astype(jnp.float32) * tok_local
    end_term = jnp.exp(-decay_rates * lag_after) * local_end
    end_share = lax.psum_scatter(end_term, "seq", scatter_dimension=1, tiled=True)
    share_cols = end_share.shape[1]
    rate_share = lax.dynamic_slice_in_dim(decay_rates, seq_index * share_cols, share_cols, 1)
    prior_share = lax.dynamic_slice_in_dim(prior_state, seq_index * share_cols, share_cols, 1)
    end_state = end_share + jnp.exp(-rate_share * float(seq_count * tok_local)) * prior_share
    return (hyena_out, end_state)


LANES = 128
SUBL = 8
MESH = pl.DeviceIdType.MESH


def one_minus_exp(y):
    series = jnp.ones_like(y)
    for k in range(9, 1, -1):
        series = 1.0 - (y / k) * series
    return jnp.where(y < 0.5, y * series, 1.0 - jnp.exp(-y))


def fused_kernel(
    n, ids_ref, emb_hbm, qkv_hbm, cw_hbm, rate_hbm, res_hbm, prior_hbm,
    out_hbm, end_ref,
    qkv_v, emb_v, cw_v, rate_v, res_v, prior_v, out_v,
    tail32, tail_send, tail_recv, ext, q_s, p_s, f_s, g_s,
    rate_r, pole_r, gain_r, rg_r, res_r, prior_r, ends, gath, pref, inc,
    load_sem, tail_sem, s1_sem, r1_sem, s2_sem, r2_sem, out_sem,
):
    members, tok, chans = qkv_v.shape
    blocks = chans // LANES
    halves = blocks // SUBL
    pitch = tok + SUBL
    modes = SUBL
    rows = blocks // n * modes
    half_cols = SUBL * LANES
    me = lax.axis_index("seq")

    loads = [
        pltpu.make_async_copy(src, dst, load_sem.at[i])
        for i, (src, dst) in enumerate(
            (
                (qkv_hbm, qkv_v),
                (rate_hbm, rate_v),
                (res_hbm, res_v),
                (prior_hbm, prior_v),
                (cw_hbm, cw_v),
                (emb_hbm, emb_v),
            )
        )
    ]
    for load in loads:
        load.start()

    barrier = pltpu.get_barrier_semaphore()
    for d in range(1, n):
        pl.semaphore_signal(
            barrier, inc=1, device_id={"seq": lax.rem(me + d, n)}, device_id_type=MESH
        )

    loads[0].wait()

    def pack_tail(b, _):
        cols = pl.ds(pl.multiple_of(b * LANES, LANES), LANES)
        for m in range(members):
            last = qkv_v[m, tok - 16 : tok, cols].astype(jnp.float32)
            tail32[pl.ds((m * blocks + b) * 2, 2), :] = last[14:16]
        return 0

    lax.fori_loop(0, blocks, pack_tail, 0, unroll=4)
    tail_send[...] = tail32[...].astype(jnp.bfloat16)
    pl.semaphore_wait(barrier, n - 1)
    tail_copy = pltpu.make_async_remote_copy(
        src_ref=tail_send,
        dst_ref=tail_recv,
        send_sem=tail_sem.at[0],
        recv_sem=tail_sem.at[1],
        device_id={"seq": lax.rem(me + 1, n)},
        device_id_type=MESH,
    )
    tail_copy.start()

    for load in loads[1:5]:
        load.wait()
    rate = rate_v[...]
    pole = jnp.exp(-rate)
    gain = jnp.sqrt(one_minus_exp(2.0 * rate))
    res = res_v[...]
    prior = prior_v[...]
    for b in range(blocks):
        cut = slice(b * LANES, (b + 1) * LANES)
        put = slice(b * modes, (b + 1) * modes)
        rate_r[put, :] = rate[:, cut]
        pole_r[put, :] = pole[:, cut]
        gain_r[put, :] = gain[:, cut]
        rg_r[put, :] = (res * gain)[:, cut]
        res_r[put, :] = res[:, cut]
        prior_r[put, :] = prior[:, cut]

    for m in range(members):
        ext[m, 0:SUBL, :] = jnp.zeros((SUBL, LANES), jnp.float32)

    def taps(m, cols):
        return [cw_v[m, j : j + 1, cols] for j in range(3)]

    def short(b, _):
        cols = pl.ds(pl.multiple_of(b * LANES, LANES), LANES)
        feats = []
        for m in range(members):
            w0, w1, w2 = taps(m, cols)
            now = qkv_v[m, :, cols].astype(jnp.float32)
            ext[m, SUBL:, :] = now
            feats.append(
                w0 * now
                + w1 * ext[m, SUBL - 1 : SUBL - 1 + tok, :]
                + w2 * ext[m, SUBL - 2 : SUBL - 2 + tok, :]
            )
        q_s[pl.ds(pl.multiple_of(b * tok, SUBL), tok), :] = feats[0]
        p_s[pl.ds(pl.multiple_of(b * pitch, SUBL), tok), :] = feats[1] * feats[2]
        return 0

    lax.fori_loop(0, blocks, short, 0)

    def per_mode(ref):
        return [
            ref[pl.ds(h * SUBL * modes + m, SUBL, stride=modes), :]
            for h in range(halves)
            for m in range(modes)
        ]

    def tokens(ref, t):
        return [ref[pl.ds(h * SUBL * pitch + t, SUBL, stride=pitch), :] for h in range(halves)]

    poles = per_mode(pole_r)

    def horner(t, state):
        now = tokens(p_s, t)
        return tuple(poles[i] * s + now[i // modes] for i, s in enumerate(state))

    zeros = tuple(jnp.zeros((SUBL, LANES), jnp.float32) for _ in range(halves * modes))
    late = lax.fori_loop(2, tok, horner, zeros, unroll=6)

    for i, s in enumerate(late):
        h, m = divmod(i, modes)
        ends[pl.ds(h * SUBL * modes + m, SUBL, stride=modes), :] = s
    tail_copy.wait_recv()
    tail32[...] = jnp.where(me > 0, tail_recv[...].astype(jnp.float32), 0.0)

    def patch(b, _):
        cols = pl.ds(pl.multiple_of(b * LANES, LANES), LANES)
        feats = []
        for m in range(members):
            w0, w1, w2 = taps(m, cols)
            now = qkv_v[m, 0:16, cols].astype(jnp.float32)[0:SUBL]
            ext[m, SUBL - 2 : SUBL, :] = tail32[pl.ds((m * blocks + b) * 2, 2), :]
            ext[m, SUBL : 2 * SUBL, :] = now
            feats.append(
                w0 * now
                + w1 * ext[m, SUBL - 1 : 2 * SUBL - 1, :]
                + w2 * ext[m, SUBL - 2 : 2 * SUBL - 2, :]
            )
        q_s[pl.ds(pl.multiple_of(b * tok, SUBL), SUBL), :] = feats[0]
        p_s[pl.ds(pl.multiple_of(b * pitch, SUBL), SUBL), :] = feats[1] * feats[2]
        return 0

    lax.fori_loop(0, blocks, patch, 0, unroll=2)
    first, second = tokens(p_s, 0), tokens(p_s, 1)
    lag = jnp.exp(-rate_r[...] * float(tok - 2))
    pref[0 : blocks * modes, :] = lag
    lags = per_mode(pref)
    gains = per_mode(gain_r)
    olds = per_mode(ends)
    for i in range(halves * modes):
        h, m = divmod(i, modes)
        early = poles[i] * first[h] + second[h]
        ends[pl.ds(h * SUBL * modes + m, SUBL, stride=modes), :] = gains[i] * (
            lags[i] * early + olds[i]
        )

    def chunk(index):
        return pl.ds(pl.multiple_of(index * rows, SUBL), rows)

    sends = []
    for d in range(1, n):
        peer = lax.rem(me + d, n)
        copy = pltpu.make_async_remote_copy(
            src_ref=ends.at[chunk(peer)],
            dst_ref=gath.at[chunk(me)],
            send_sem=s1_sem.at[d],
            recv_sem=r1_sem.at[d],
            device_id={"seq": peer},
            device_id_type=MESH,
        )
        copy.start()
        sends.append(copy)
    gath[chunk(me), :] = ends[chunk(me), :]

    weights = per_mode(rg_r)

    def scan(t, state):
        now = tokens(p_s, t)
        state = tuple(poles[i] * s + now[i // modes] for i, s in enumerate(state))
        for h in range(halves):
            terms = [weights[i] * state[i] for i in range(h * modes, (h + 1) * modes)]
            while len(terms) > 1:
                terms = [a + b for a, b in zip(terms[::2], terms[1::2])]
            f_s[pl.ds(h * SUBL * pitch + t, SUBL, stride=pitch), :] = terms[0]
        return state

    lax.fori_loop(0, tok, scan, zeros, unroll=4)

    for copy in sends:
        copy.wait_recv()
    step = jnp.exp(-rate_r[chunk(me), :] * float(tok))
    state = prior_r[chunk(me), :]
    for copy in sends:
        copy.wait_send()
    for i in range(n):
        pref[i * rows : (i + 1) * rows, :] = state
        state = step * state + gath[i * rows : (i + 1) * rows, :]

    returns = []
    for d in range(1, n):
        peer = lax.rem(me + d, n)
        copy = pltpu.make_async_remote_copy(
            src_ref=pref.at[chunk(peer)],
            dst_ref=inc.at[chunk(me)],
            send_sem=s2_sem.at[d],
            recv_sem=r2_sem.at[d],
            device_id={"seq": peer},
            device_id_type=MESH,
        )
        copy.start()
        returns.append(copy)
    inc[chunk(me), :] = pref[chunk(me), :]
    for b in range(rows // modes):
        end_ref[:, b * LANES : (b + 1) * LANES] = state[b * modes : (b + 1) * modes]

    loads[5].wait()
    vocab = emb_v.shape[0]
    which = lax.broadcasted_iota(jnp.int32, (vocab, tok), 0) == ids_ref[...]
    one_hot = jnp.where(which, 1.0, 0.0).astype(jnp.bfloat16)
    wide = 2 * LANES

    def embed(b, _):
        cols = pl.ds(pl.multiple_of(b * wide, wide), wide)
        g_s[:, cols] = lax.dot_general(
            one_hot, emb_v[:, cols], (((0,), (0,)), ((), ())),
            preferred_element_type=jnp.float32,
        )
        return 0

    lax.fori_loop(0, chans // wide, embed, 0)

    for copy in returns:
        copy.wait_recv()
    inc[...] = res_r[...] * inc[...]
    shares = per_mode(inc)
    stores = []
    for h in range(halves):
        half_poles = poles[h * modes : (h + 1) * modes]

        def carried(t, share, h=h, half_poles=half_poles):
            share = tuple(p * s for p, s in zip(half_poles, share))
            terms = list(share)
            while len(terms) > 1:
                terms = [a + b for a, b in zip(terms[::2], terms[1::2])]
            spot = pl.ds(h * SUBL * pitch + t, SUBL, stride=pitch)
            f_s[spot, :] = f_s[spot, :] + terms[0]
            return share

        lax.fori_loop(
            0, tok, carried, tuple(shares[h * modes : (h + 1) * modes]), unroll=8
        )

        def finish(b, _):
            cols = pl.ds(pl.multiple_of(b * LANES, LANES), LANES)
            filtered = f_s[pl.ds(pl.multiple_of(b * pitch, SUBL), tok), :]
            q_feat = q_s[pl.ds(pl.multiple_of(b * tok, SUBL), tok), :]
            out_v[:, cols] = (g_s[:, cols] + q_feat * filtered).astype(jnp.bfloat16)
            return 0

        lax.fori_loop(h * SUBL, (h + 1) * SUBL, finish, 0)
        span = pl.ds(h * half_cols, half_cols)
        store = pltpu.make_async_copy(out_v.at[:, span], out_hbm.at[:, span], out_sem.at[h])
        store.start()
        stores.append(store)
    tail_copy.wait_send()
    for copy in returns:
        copy.wait_send()
    for store in stores:
        store.wait()


def fused_body(token_ids, embed_table, hyena_qkv, conv_weights, decay_rates, residues, prior_state):
    n = lax.axis_size("seq")
    members, tok, chans = hyena_qkv.shape
    modes = decay_rates.shape[0]
    blocks = chans // LANES
    table = pltpu.VMEM((blocks * modes, LANES), jnp.float32)
    f32 = jnp.float32
    padded = blocks * (tok + SUBL)
    scratch = [
        pltpu.VMEM(hyena_qkv.shape, jnp.bfloat16),
        pltpu.VMEM(embed_table.shape, jnp.bfloat16),
        pltpu.VMEM(conv_weights.shape, f32),
        pltpu.VMEM(decay_rates.shape, f32),
        pltpu.VMEM(residues.shape, f32),
        pltpu.VMEM(prior_state.shape, f32),
        pltpu.VMEM((tok, chans), jnp.bfloat16),
        pltpu.VMEM((members * blocks * 2, LANES), f32),
        pltpu.VMEM((members * blocks * 2, LANES), jnp.bfloat16),
        pltpu.VMEM((members * blocks * 2, LANES), jnp.bfloat16),
        pltpu.VMEM((members, tok + SUBL, LANES), f32),
        pltpu.VMEM((blocks * tok, LANES), f32),
        pltpu.VMEM((padded, LANES), f32),
        pltpu.VMEM((padded, LANES), f32),
        pltpu.VMEM((tok, chans), f32),
    ] + [table] * 10 + [
        pltpu.SemaphoreType.DMA((6,)),
        pltpu.SemaphoreType.DMA((2,)),
    ] + [pltpu.SemaphoreType.DMA((n,))] * 4 + [
        pltpu.SemaphoreType.DMA((blocks // SUBL,)),
    ]
    any_spec = pl.BlockSpec(memory_space=pl.ANY)
    vmem_spec = pl.BlockSpec(memory_space=pltpu.VMEM)
    return pl.pallas_call(
        functools.partial(fused_kernel, n),
        out_shape=(
            jax.ShapeDtypeStruct((tok, chans), jnp.bfloat16),
            jax.ShapeDtypeStruct((modes, chans // n), f32),
        ),
        in_specs=[vmem_spec] + [any_spec] * 6,
        out_specs=(any_spec, vmem_spec),
        scratch_shapes=scratch,
        compiler_params=pltpu.CompilerParams(
            collective_id=0, has_side_effects=True, vmem_limit_bytes=40 * 1024 * 1024
        ),
    )(
        token_ids.reshape(1, tok), embed_table, hyena_qkv, conv_weights,
        decay_rates, residues, prior_state,
    )


def body(token_ids, embed_table, hyena_qkv, conv_weights, decay_rates, residues, prior_state):
    n = lax.axis_size("seq")
    members, tok, chans = hyena_qkv.shape
    fits = (
        chans % (n * LANES) == 0
        and chans % (SUBL * LANES) == 0
        and tok % LANES == 0
        and decay_rates.shape[0] == SUBL
        and conv_weights.shape[1] == 3
    )
    run = fused_body if fits else plain_body
    return run(
        token_ids, embed_table, hyena_qkv, conv_weights, decay_rates, residues, prior_state
    )


def solution(mesh):
    return jax.shard_map(
        body,
        mesh=mesh,
        in_specs=(
            P(("groups", "seq")),
            P(None, "tp"),
            P(None, ("groups", "seq"), "tp"),
            P(None, None, "tp"),
            P(None, "tp"),
            P(None, "tp"),
            P("groups", "tp"),
        ),
        out_specs=(P(("groups", "seq"), "tp"), P("groups", ("tp", "seq"))),
        check_vma=False,
    )
```

```python
import functools
import jax
import jax.numpy as jnp
from jax import lax
from jax.experimental import pallas as pl
from jax.experimental.pallas import tpu as pltpu
from jax.sharding import PartitionSpec as P


def shifted(array, axis, by):
    size = lax.axis_size(axis)
    pairs = [(i, i + by) for i in range(size) if 0 <= i + by < size]
    return lax.ppermute(array, axis, pairs)


def short_features(extended, conv_weights, tok_local):
    tap_count = conv_weights.shape[1]
    results = []
    for member in range(3):
        total = jnp.zeros((tok_local, extended.shape[2]), jnp.float32)
        for tap_index in range(tap_count):
            offset = tap_count - 1 - tap_index
            total = total + conv_weights[member, tap_index][None, :] * extended[
                member, offset : offset + tok_local
            ].astype(jnp.float32)
        results.append(total)
    return results


def modal_local(product_in, decay_rates, residues, sub_len):
    tok_local, channels = product_in.shape
    block_count = tok_local // sub_len
    blocks = product_in.reshape(block_count, sub_len, channels)
    spacing = jnp.arange(sub_len, dtype=jnp.float32)
    gain = jnp.sqrt(-jnp.expm1(-2.0 * decay_rates))
    decay_table = jnp.exp(-decay_rates[:, None, :] * spacing[None, :, None])
    kernel = jnp.sum((residues * gain)[:, None, :] * decay_table, axis=0)
    extended = jnp.concatenate(
        [kernel[::-1], jnp.zeros((sub_len - 1, channels), jnp.float32)], axis=0
    )
    toeplitz = jnp.stack(
        [extended[sub_len - 1 - row : 2 * sub_len - 1 - row] for row in range(sub_len)], axis=0
    )
    inner = jnp.einsum("tsc,bsc->btc", toeplitz, blocks, precision=lax.Precision.HIGHEST)
    tail_weight = gain[:, None, :] * jnp.exp(
        -decay_rates[:, None, :] * (sub_len - 1 - spacing)[None, :, None]
    )
    closing = jnp.einsum("bsc,msc->bmc", blocks, tail_weight, precision=lax.Precision.HIGHEST)
    per_block = jnp.exp(-decay_rates * sub_len)

    def advance(carry, piece):
        return (per_block * carry + piece, carry)

    local_end, starts = lax.scan(advance, jnp.zeros_like(decay_rates), closing)
    return (inner, starts, local_end)


def modal_readout(inner, starts, incoming, decay_rates, residues, sub_len):
    block_count = starts.shape[0]
    block_pos = jnp.arange(block_count, dtype=jnp.float32) * sub_len
    opening = (
        starts + jnp.exp(-decay_rates[None, :, :] * block_pos[:, None, None]) * incoming[None, :, :]
    )
    spacing = jnp.arange(sub_len, dtype=jnp.float32)
    readout = residues[:, None, :] * jnp.exp(
        -decay_rates[:, None, :] * (spacing + 1.0)[None, :, None]
    )
    outer = jnp.einsum("bmc,mtc->btc", opening, readout, precision=lax.Precision.HIGHEST)
    return (inner + outer).reshape(block_count * sub_len, inner.shape[2])


def plain_body(token_ids, embed_table, hyena_qkv, conv_weights, decay_rates, residues, prior_state):
    tok_local = hyena_qkv.shape[1]
    tap_count = conv_weights.shape[1]
    seq_count = lax.axis_size("seq")
    seq_index = lax.axis_index("seq")
    tails_local = hyena_qkv[:, tok_local - (tap_count - 1) :, :]
    tails_prev = shifted(tails_local, "seq", 1)
    extended = jnp.concatenate([tails_prev, hyena_qkv], axis=1)
    q_feat, k_feat, v_feat = short_features(extended, conv_weights, tok_local)
    product_in = k_feat * v_feat
    sub_len = 16
    inner, starts, local_end = modal_local(product_in, decay_rates, residues, sub_len)
    piece = lax.all_gather(local_end[None], "seq", axis=0, tiled=True)
    count = piece.shape[0]
    sources = jnp.arange(count, dtype=jnp.int32)
    gap_len = jnp.maximum(seq_index - 1 - sources, 0).astype(jnp.float32) * tok_local
    factors = jnp.where(
        (sources < seq_index)[:, None, None],
        jnp.exp(-decay_rates[None, :, :] * gap_len[:, None, None]),
        0.0,
    )
    folded = jnp.sum(factors * piece, axis=0)
    incoming = (
        folded + jnp.exp(-decay_rates * (seq_index.astype(jnp.float32) * tok_local)) * prior_state
    )
    filtered = modal_readout(inner, starts, incoming, decay_rates, residues, sub_len)
    vocab_ids = jnp.arange(embed_table.shape[0], dtype=jnp.int32)
    one_hot = (token_ids[:, None] == vocab_ids[None, :]).astype(jnp.bfloat16)
    embedded = jnp.dot(one_hot, embed_table, preferred_element_type=jnp.float32)
    hyena_out = (embedded + q_feat * filtered).astype(jnp.bfloat16)
    lag_after = (seq_count - 1 - seq_index).astype(jnp.float32) * tok_local
    end_term = jnp.exp(-decay_rates * lag_after) * local_end
    end_share = lax.psum_scatter(end_term, "seq", scatter_dimension=1, tiled=True)
    share_cols = end_share.shape[1]
    rate_share = lax.dynamic_slice_in_dim(decay_rates, seq_index * share_cols, share_cols, 1)
    prior_share = lax.dynamic_slice_in_dim(prior_state, seq_index * share_cols, share_cols, 1)
    end_state = end_share + jnp.exp(-rate_share * float(seq_count * tok_local)) * prior_share
    return (hyena_out, end_state)


LANES = 128
SUBL = 8
MESH = pl.DeviceIdType.MESH


def one_minus_exp(y):
    series = jnp.ones_like(y)
    for k in range(9, 1, -1):
        series = 1.0 - (y / k) * series
    return jnp.where(y < 0.5, y * series, 1.0 - jnp.exp(-y))


def fused_kernel(
    n, ids_ref, emb_hbm, qkv_hbm, cw_hbm, rate_hbm, res_hbm, prior_hbm,
    inc_hbm, table_hbm, q_hbm, base_hbm, end_hbm,
    qkv_v, emb_v, cw_v, rate_v, res_v, prior_v,
    tail32, tail_send, tail_recv, ext, q_s, p_s, f_s, base_v, end_v, table_v,
    rate_r, gain_r, rg_r, prior_r, ends, gath, pref,
    load_sem, tail_sem, s1_sem, r1_sem, s2_sem, r2_sem, store_sem,
):
    members, tok, chans = qkv_v.shape
    blocks = chans // LANES
    halves = blocks // SUBL
    pitch = tok + SUBL
    modes = SUBL
    rows = blocks // n * modes
    me = lax.axis_index("seq")

    loads = [
        pltpu.make_async_copy(src, dst, load_sem.at[i])
        for i, (src, dst) in enumerate(
            (
                (qkv_hbm, qkv_v),
                (rate_hbm, rate_v),
                (res_hbm, res_v),
                (prior_hbm, prior_v),
                (cw_hbm, cw_v),
                (emb_hbm, emb_v),
            )
        )
    ]
    for load in loads:
        load.start()

    barrier = pltpu.get_barrier_semaphore()
    for d in range(1, n):
        pl.semaphore_signal(
            barrier, inc=1, device_id={"seq": lax.rem(me + d, n)}, device_id_type=MESH
        )

    loads[0].wait()

    def pack_tail(b, _):
        cols = pl.ds(pl.multiple_of(b * LANES, LANES), LANES)
        for m in range(members):
            last = qkv_v[m, tok - 16 : tok, cols].astype(jnp.float32)
            tail32[pl.ds((m * blocks + b) * 2, 2), :] = last[14:16]
        return 0

    lax.fori_loop(0, blocks, pack_tail, 0, unroll=4)
    tail_send[...] = tail32[...].astype(jnp.bfloat16)
    pl.semaphore_wait(barrier, n - 1)
    tail_copy = pltpu.make_async_remote_copy(
        src_ref=tail_send,
        dst_ref=tail_recv,
        send_sem=tail_sem.at[0],
        recv_sem=tail_sem.at[1],
        device_id={"seq": lax.rem(me + 1, n)},
        device_id_type=MESH,
    )
    tail_copy.start()

    for load in loads[1:5]:
        load.wait()
    rate = rate_v[...]
    pole = jnp.exp(-rate)
    gain = jnp.sqrt(one_minus_exp(2.0 * rate))
    res = res_v[...]
    prior = prior_v[...]
    for b in range(blocks):
        cut = slice(b * LANES, (b + 1) * LANES)
        put = slice(b * modes, (b + 1) * modes)
        rate_r[put, :] = rate[:, cut]
        table_v[0, put, :] = pole[:, cut]
        gain_r[put, :] = gain[:, cut]
        rg_r[put, :] = (res * gain)[:, cut]
        table_v[1, put, :] = res[:, cut]
        prior_r[put, :] = prior[:, cut]
    stores = [pltpu.make_async_copy(table_v, table_hbm, store_sem.at[0])]
    stores[0].start()

    for m in range(members):
        ext[m, 0:SUBL, :] = jnp.zeros((SUBL, LANES), jnp.float32)

    def taps(m, cols):
        return [cw_v[m, j : j + 1, cols] for j in range(3)]

    def filtered_block(m, cols):
        w0, w1, w2 = taps(m, cols)
        now = qkv_v[m, :, cols].astype(jnp.float32)
        ext[m, SUBL:, :] = now
        return (
            w0 * now
            + w1 * ext[m, SUBL - 1 : SUBL - 1 + tok, :]
            + w2 * ext[m, SUBL - 2 : SUBL - 2 + tok, :]
        )

    def short(b, _):
        cols = pl.ds(pl.multiple_of(b * LANES, LANES), LANES)
        k_feat, v_feat = [filtered_block(m, cols) for m in (1, 2)]
        p_s[pl.ds(pl.multiple_of(b * pitch, SUBL), tok), :] = k_feat * v_feat
        return 0

    lax.fori_loop(0, blocks, short, 0)

    def per_mode(ref):
        return [
            ref[pl.ds(h * SUBL * modes + m, SUBL, stride=modes), :]
            for h in range(halves)
            for m in range(modes)
        ]

    def tokens(ref, t):
        return [ref[pl.ds(h * SUBL * pitch + t, SUBL, stride=pitch), :] for h in range(halves)]

    poles = per_mode(table_v.at[0])

    def horner(t, state):
        now = tokens(p_s, t)
        return tuple(poles[i] * s + now[i // modes] for i, s in enumerate(state))

    zeros = tuple(jnp.zeros((SUBL, LANES), jnp.float32) for _ in range(halves * modes))
    late = lax.fori_loop(2, tok, horner, zeros, unroll=6)

    for i, s in enumerate(late):
        h, m = divmod(i, modes)
        ends[pl.ds(h * SUBL * modes + m, SUBL, stride=modes), :] = s
    tail_copy.wait_recv()
    tail32[...] = jnp.where(me > 0, tail_recv[...].astype(jnp.float32), 0.0)

    def patch(b, _):
        cols = pl.ds(pl.multiple_of(b * LANES, LANES), LANES)
        feats = []
        for m in (1, 2):
            w0, w1, w2 = taps(m, cols)
            now = qkv_v[m, 0:16, cols].astype(jnp.float32)[0:SUBL]
            ext[m, SUBL - 2 : SUBL, :] = tail32[pl.ds((m * blocks + b) * 2, 2), :]
            ext[m, SUBL : 2 * SUBL, :] = now
            feats.append(
                w0 * now
                + w1 * ext[m, SUBL - 1 : 2 * SUBL - 1, :]
                + w2 * ext[m, SUBL - 2 : 2 * SUBL - 2, :]
            )
        p_s[pl.ds(pl.multiple_of(b * pitch, SUBL), SUBL), :] = feats[0] * feats[1]
        return 0

    lax.fori_loop(0, blocks, patch, 0, unroll=2)
    first, second = tokens(p_s, 0), tokens(p_s, 1)
    lag = jnp.exp(-rate_r[...] * float(tok - 2))
    pref[0 : blocks * modes, :] = lag
    lags = per_mode(pref)
    gains = per_mode(gain_r)
    olds = per_mode(ends)
    for i in range(halves * modes):
        h, m = divmod(i, modes)
        early = poles[i] * first[h] + second[h]
        ends[pl.ds(h * SUBL * modes + m, SUBL, stride=modes), :] = gains[i] * (
            lags[i] * early + olds[i]
        )

    def chunk(index):
        return pl.ds(pl.multiple_of(index * rows, SUBL), rows)

    sends = []
    for d in range(1, n):
        peer = lax.rem(me + d, n)
        copy = pltpu.make_async_remote_copy(
            src_ref=ends.at[chunk(peer)],
            dst_ref=gath.at[chunk(me)],
            send_sem=s1_sem.at[d],
            recv_sem=r1_sem.at[d],
            device_id={"seq": peer},
            device_id_type=MESH,
        )
        copy.start()
        sends.append(copy)
    gath[chunk(me), :] = ends[chunk(me), :]

    weights = per_mode(rg_r)

    def scan(t, state):
        now = tokens(p_s, t)
        state = tuple(poles[i] * s + now[i // modes] for i, s in enumerate(state))
        for h in range(halves):
            terms = [weights[i] * state[i] for i in range(h * modes, (h + 1) * modes)]
            while len(terms) > 1:
                terms = [a + b for a, b in zip(terms[::2], terms[1::2])]
            f_s[pl.ds(h * SUBL * pitch + t, SUBL, stride=pitch), :] = terms[0]
        return state

    lax.fori_loop(0, tok, scan, zeros, unroll=4)

    def query(b, _):
        cols = pl.ds(pl.multiple_of(b * LANES, LANES), LANES)
        ext[0, SUBL - 2 : SUBL, :] = tail32[pl.ds(b * 2, 2), :]
        q_s[:, cols] = filtered_block(0, cols)
        return 0

    lax.fori_loop(0, blocks, query, 0)
    stores.append(pltpu.make_async_copy(q_s, q_hbm, store_sem.at[1]))
    stores[1].start()

    for copy in sends:
        copy.wait_recv()
    step = jnp.exp(-rate_r[chunk(me), :] * float(tok))
    state = prior_r[chunk(me), :]
    for copy in sends:
        copy.wait_send()
    for i in range(n):
        pref[i * rows : (i + 1) * rows, :] = state
        state = step * state + gath[i * rows : (i + 1) * rows, :]

    returns = []
    for d in range(1, n):
        peer = lax.rem(me + d, n)
        copy = pltpu.make_async_remote_copy(
            src_ref=pref.at[chunk(peer)],
            dst_ref=inc_hbm.at[chunk(me)],
            send_sem=s2_sem.at[d],
            recv_sem=r2_sem.at[d],
            device_id={"seq": peer},
            device_id_type=MESH,
        )
        copy.start()
        returns.append(copy)
    stores.append(
        pltpu.make_async_copy(pref.at[chunk(me)], inc_hbm.at[chunk(me)], store_sem.at[2])
    )
    stores[2].start()
    for b in range(rows // modes):
        end_v[:, b * LANES : (b + 1) * LANES] = state[b * modes : (b + 1) * modes]
    stores.append(pltpu.make_async_copy(end_v, end_hbm, store_sem.at[3]))
    stores[3].start()

    loads[5].wait()
    vocab = emb_v.shape[0]
    which = lax.broadcasted_iota(jnp.int32, (vocab, tok), 0) == ids_ref[...]
    one_hot = jnp.where(which, 1.0, 0.0).astype(jnp.bfloat16)
    wide = 2 * LANES

    def embed(b, _):
        cols = pl.ds(pl.multiple_of(b * wide, wide), wide)
        embedded = lax.dot_general(
            one_hot, emb_v[:, cols], (((0,), (0,)), ((), ())),
            preferred_element_type=jnp.float32,
        )
        for i in range(2):
            part = pl.ds(pl.multiple_of((b * 2 + i) * LANES, LANES), LANES)
            filtered = f_s[pl.ds(pl.multiple_of((b * 2 + i) * pitch, SUBL), tok), :]
            base_v[:, part] = (
                embedded[:, i * LANES : (i + 1) * LANES] + q_s[:, part] * filtered
            )
        return 0

    lax.fori_loop(0, chans // wide, embed, 0)
    stores.append(pltpu.make_async_copy(base_v, base_hbm, store_sem.at[4]))
    stores[4].start()

    tail_copy.wait_send()
    for copy in returns:
        copy.wait_send()
    for store in stores:
        store.wait()
    for copy in returns:
        copy.wait_recv()


def finish_kernel(
    inc_hbm, table_hbm, q_hbm, base_hbm, end_hbm,
    out_hbm, end_out,
    inc, table_v, q_v, base_v, end_v, f_s, out_v,
    load_sem, store_sem,
):
    tok, chans = q_v.shape
    blocks = chans // LANES
    halves = blocks // SUBL
    pitch = tok + SUBL
    modes = SUBL
    half_cols = SUBL * LANES
    loads = [
        pltpu.make_async_copy(src, dst, load_sem.at[i])
        for i, (src, dst) in enumerate(
            (
                (inc_hbm, inc),
                (table_hbm, table_v),
                (end_hbm, end_v),
                (q_hbm, q_v),
                (base_hbm, base_v),
            )
        )
    ]
    for load in loads:
        load.start()
    for load in loads[:2]:
        load.wait()
    inc[...] = table_v[1] * inc[...]
    stores = []
    for h in range(halves):
        spots = [pl.ds(h * SUBL * modes + m, SUBL, stride=modes) for m in range(modes)]
        poles = [table_v.at[0][spot, :] for spot in spots]
        shares = tuple(inc[spot, :] for spot in spots)

        def carried(t, share, h=h, poles=poles):
            share = tuple(p * s for p, s in zip(poles, share))
            terms = list(share)
            while len(terms) > 1:
                terms = [a + b for a, b in zip(terms[::2], terms[1::2])]
            f_s[pl.ds(h * SUBL * pitch + t, SUBL, stride=pitch), :] = terms[0]
            return share

        lax.fori_loop(0, tok, carried, shares, unroll=8)
        if h == 0:
            loads[2].wait()
            stores.append(pltpu.make_async_copy(end_v, end_out, store_sem.at[halves]))
            stores[0].start()
            loads[3].wait()
            loads[4].wait()

        def finish(b, _):
            cols = pl.ds(pl.multiple_of(b * LANES, LANES), LANES)
            filtered = f_s[pl.ds(pl.multiple_of(b * pitch, SUBL), tok), :]
            out_v[:, cols] = (base_v[:, cols] + q_v[:, cols] * filtered).astype(jnp.bfloat16)
            return 0

        lax.fori_loop(h * SUBL, (h + 1) * SUBL, finish, 0)
        span = pl.ds(h * half_cols, half_cols)
        store = pltpu.make_async_copy(out_v.at[:, span], out_hbm.at[:, span], store_sem.at[h])
        store.start()
        stores.append(store)
    for store in stores:
        store.wait()


def fused_body(token_ids, embed_table, hyena_qkv, conv_weights, decay_rates, residues, prior_state):
    n = lax.axis_size("seq")
    members, tok, chans = hyena_qkv.shape
    modes = decay_rates.shape[0]
    blocks = chans // LANES
    f32 = jnp.float32
    rows = blocks * modes
    table = pltpu.VMEM((rows, LANES), f32)
    padded = pltpu.VMEM((blocks * (tok + SUBL), LANES), f32)
    whole = pltpu.VMEM((tok, chans), f32)
    packed = (members * blocks * 2, LANES)
    end_shape = (modes, chans // n)
    scratch = [
        pltpu.VMEM(hyena_qkv.shape, jnp.bfloat16),
        pltpu.VMEM(embed_table.shape, jnp.bfloat16),
        pltpu.VMEM(conv_weights.shape, f32),
        pltpu.VMEM(decay_rates.shape, f32),
        pltpu.VMEM(residues.shape, f32),
        pltpu.VMEM(prior_state.shape, f32),
        pltpu.VMEM(packed, f32),
        pltpu.VMEM(packed, jnp.bfloat16),
        pltpu.VMEM(packed, jnp.bfloat16),
        pltpu.VMEM((members, tok + SUBL, LANES), f32),
        whole,
        padded,
        padded,
        whole,
        pltpu.VMEM(end_shape, f32),
        pltpu.VMEM((2, rows, LANES), f32),
    ] + [table] * 7 + [
        pltpu.SemaphoreType.DMA((6,)),
        pltpu.SemaphoreType.DMA((2,)),
    ] + [pltpu.SemaphoreType.DMA((n,))] * 4 + [pltpu.SemaphoreType.DMA((5,))]
    hbm_spec = pl.BlockSpec(memory_space=pltpu.HBM)
    vmem_spec = pl.BlockSpec(memory_space=pltpu.VMEM)
    room = 60 * 1024 * 1024
    parts = pl.pallas_call(
        functools.partial(fused_kernel, n),
        out_shape=(
            jax.ShapeDtypeStruct((rows, LANES), f32),
            jax.ShapeDtypeStruct((2, rows, LANES), f32),
            jax.ShapeDtypeStruct((tok, chans), f32),
            jax.ShapeDtypeStruct((tok, chans), f32),
            jax.ShapeDtypeStruct(end_shape, f32),
        ),
        in_specs=[vmem_spec] + [hbm_spec] * 6,
        out_specs=(hbm_spec,) * 5,
        scratch_shapes=scratch,
        compiler_params=pltpu.CompilerParams(
            collective_id=0, has_side_effects=True, vmem_limit_bytes=room
        ),
    )(
        token_ids.reshape(1, tok), embed_table, hyena_qkv, conv_weights,
        decay_rates, residues, prior_state,
    )
    return pl.pallas_call(
        finish_kernel,
        out_shape=(
            jax.ShapeDtypeStruct((tok, chans), jnp.bfloat16),
            jax.ShapeDtypeStruct(end_shape, f32),
        ),
        in_specs=[hbm_spec] * 5,
        out_specs=(hbm_spec,) * 2,
        scratch_shapes=[
            table,
            pltpu.VMEM((2, rows, LANES), f32),
            whole,
            whole,
            pltpu.VMEM(end_shape, f32),
            padded,
            pltpu.VMEM((tok, chans), jnp.bfloat16),
            pltpu.SemaphoreType.DMA((5,)),
            pltpu.SemaphoreType.DMA((blocks // SUBL + 1,)),
        ],
        compiler_params=pltpu.CompilerParams(vmem_limit_bytes=room),
    )(*parts)


def body(token_ids, embed_table, hyena_qkv, conv_weights, decay_rates, residues, prior_state):
    n = lax.axis_size("seq")
    members, tok, chans = hyena_qkv.shape
    fits = (
        chans % (n * LANES) == 0
        and chans % (SUBL * LANES) == 0
        and tok % LANES == 0
        and decay_rates.shape[0] == SUBL
        and conv_weights.shape[1] == 3
    )
    run = fused_body if fits else plain_body
    return run(
        token_ids, embed_table, hyena_qkv, conv_weights, decay_rates, residues, prior_state
    )


def solution(mesh):
    return jax.shard_map(
        body,
        mesh=mesh,
        in_specs=(
            P(("groups", "seq")),
            P(None, "tp"),
            P(None, ("groups", "seq"), "tp"),
            P(None, None, "tp"),
            P(None, "tp"),
            P(None, "tp"),
            P("groups", "tp"),
        ),
        out_specs=(P(("groups", "seq"), "tp"), P("groups", ("tp", "seq"))),
        check_vma=False,
    )
```

```python
import functools
import jax
import jax.numpy as jnp
from jax import lax
from jax.experimental import pallas as pl
from jax.experimental.pallas import tpu as pltpu
from jax.sharding import PartitionSpec as P


def shifted(array, axis, by):
    size = lax.axis_size(axis)
    pairs = [(i, i + by) for i in range(size) if 0 <= i + by < size]
    return lax.ppermute(array, axis, pairs)


def short_features(extended, conv_weights, tok_local):
    tap_count = conv_weights.shape[1]
    results = []
    for member in range(3):
        total = jnp.zeros((tok_local, extended.shape[2]), jnp.float32)
        for tap_index in range(tap_count):
            offset = tap_count - 1 - tap_index
            total = total + conv_weights[member, tap_index][None, :] * extended[
                member, offset : offset + tok_local
            ].astype(jnp.float32)
        results.append(total)
    return results


def modal_local(product_in, decay_rates, residues, sub_len):
    tok_local, channels = product_in.shape
    block_count = tok_local // sub_len
    blocks = product_in.reshape(block_count, sub_len, channels)
    spacing = jnp.arange(sub_len, dtype=jnp.float32)
    gain = jnp.sqrt(-jnp.expm1(-2.0 * decay_rates))
    decay_table = jnp.exp(-decay_rates[:, None, :] * spacing[None, :, None])
    kernel = jnp.sum((residues * gain)[:, None, :] * decay_table, axis=0)
    extended = jnp.concatenate(
        [kernel[::-1], jnp.zeros((sub_len - 1, channels), jnp.float32)], axis=0
    )
    toeplitz = jnp.stack(
        [extended[sub_len - 1 - row : 2 * sub_len - 1 - row] for row in range(sub_len)], axis=0
    )
    inner = jnp.einsum("tsc,bsc->btc", toeplitz, blocks, precision=lax.Precision.HIGHEST)
    tail_weight = gain[:, None, :] * jnp.exp(
        -decay_rates[:, None, :] * (sub_len - 1 - spacing)[None, :, None]
    )
    closing = jnp.einsum("bsc,msc->bmc", blocks, tail_weight, precision=lax.Precision.HIGHEST)
    per_block = jnp.exp(-decay_rates * sub_len)

    def advance(carry, piece):
        return (per_block * carry + piece, carry)

    local_end, starts = lax.scan(advance, jnp.zeros_like(decay_rates), closing)
    return (inner, starts, local_end)


def modal_readout(inner, starts, incoming, decay_rates, residues, sub_len):
    block_count = starts.shape[0]
    block_pos = jnp.arange(block_count, dtype=jnp.float32) * sub_len
    opening = (
        starts + jnp.exp(-decay_rates[None, :, :] * block_pos[:, None, None]) * incoming[None, :, :]
    )
    spacing = jnp.arange(sub_len, dtype=jnp.float32)
    readout = residues[:, None, :] * jnp.exp(
        -decay_rates[:, None, :] * (spacing + 1.0)[None, :, None]
    )
    outer = jnp.einsum("bmc,mtc->btc", opening, readout, precision=lax.Precision.HIGHEST)
    return (inner + outer).reshape(block_count * sub_len, inner.shape[2])


def plain_body(token_ids, embed_table, hyena_qkv, conv_weights, decay_rates, residues, prior_state):
    tok_local = hyena_qkv.shape[1]
    tap_count = conv_weights.shape[1]
    seq_count = lax.axis_size("seq")
    seq_index = lax.axis_index("seq")
    tails_local = hyena_qkv[:, tok_local - (tap_count - 1) :, :]
    tails_prev = shifted(tails_local, "seq", 1)
    extended = jnp.concatenate([tails_prev, hyena_qkv], axis=1)
    q_feat, k_feat, v_feat = short_features(extended, conv_weights, tok_local)
    product_in = k_feat * v_feat
    sub_len = 16
    inner, starts, local_end = modal_local(product_in, decay_rates, residues, sub_len)
    piece = lax.all_gather(local_end[None], "seq", axis=0, tiled=True)
    count = piece.shape[0]
    sources = jnp.arange(count, dtype=jnp.int32)
    gap_len = jnp.maximum(seq_index - 1 - sources, 0).astype(jnp.float32) * tok_local
    factors = jnp.where(
        (sources < seq_index)[:, None, None],
        jnp.exp(-decay_rates[None, :, :] * gap_len[:, None, None]),
        0.0,
    )
    folded = jnp.sum(factors * piece, axis=0)
    incoming = (
        folded + jnp.exp(-decay_rates * (seq_index.astype(jnp.float32) * tok_local)) * prior_state
    )
    filtered = modal_readout(inner, starts, incoming, decay_rates, residues, sub_len)
    vocab_ids = jnp.arange(embed_table.shape[0], dtype=jnp.int32)
    one_hot = (token_ids[:, None] == vocab_ids[None, :]).astype(jnp.bfloat16)
    embedded = jnp.dot(one_hot, embed_table, preferred_element_type=jnp.float32)
    hyena_out = (embedded + q_feat * filtered).astype(jnp.bfloat16)
    lag_after = (seq_count - 1 - seq_index).astype(jnp.float32) * tok_local
    end_term = jnp.exp(-decay_rates * lag_after) * local_end
    end_share = lax.psum_scatter(end_term, "seq", scatter_dimension=1, tiled=True)
    share_cols = end_share.shape[1]
    rate_share = lax.dynamic_slice_in_dim(decay_rates, seq_index * share_cols, share_cols, 1)
    prior_share = lax.dynamic_slice_in_dim(prior_state, seq_index * share_cols, share_cols, 1)
    end_state = end_share + jnp.exp(-rate_share * float(seq_count * tok_local)) * prior_share
    return (hyena_out, end_state)


LANES = 128
SUBL = 8
MESH = pl.DeviceIdType.MESH


def one_minus_exp(y):
    series = jnp.ones_like(y)
    for k in range(9, 1, -1):
        series = 1.0 - (y / k) * series
    return jnp.where(y < 0.5, y * series, 1.0 - jnp.exp(-y))


def fused_kernel(
    n, ids_ref, emb_hbm, qkv_hbm, cw_hbm, rate_hbm, res_hbm, prior_hbm,
    inc_hbm, table_hbm, q_hbm, base_hbm, end_hbm,
    qkv_v, emb_v, cw_v, rate_v, res_v, prior_v,
    tail32, tail_send, tail_recv, ext, q_s, p_s, f_s, base_v, end_v, table_v,
    rate_r, gain_r, rg_r, prior_r, ends, gath, pref,
    load_sem, tail_sem, s1_sem, r1_sem, s2_sem, r2_sem, store_sem,
):
    members, tok, chans = qkv_v.shape
    blocks = chans // LANES
    halves = blocks // SUBL
    pitch = tok + SUBL
    modes = SUBL
    rows = blocks // n * modes
    me = lax.axis_index("seq")

    barrier = pltpu.get_barrier_semaphore()
    for d in range(1, n):
        pl.semaphore_signal(
            barrier, inc=1, device_id={"seq": lax.rem(me + d, n)}, device_id_type=MESH
        )

    loads = [
        pltpu.make_async_copy(src, dst, load_sem.at[i])
        for i, (src, dst) in enumerate(
            (
                (qkv_hbm, qkv_v),
                (rate_hbm, rate_v),
                (res_hbm, res_v),
                (prior_hbm, prior_v),
                (cw_hbm, cw_v),
                (emb_hbm, emb_v),
            )
        )
    ]
    for load in loads:
        load.start()

    loads[0].wait()

    def pack_tail(b, _):
        cols = pl.ds(pl.multiple_of(b * LANES, LANES), LANES)
        for m in range(members):
            last = qkv_v[m, tok - 16 : tok, cols].astype(jnp.float32)
            tail32[pl.ds((m * blocks + b) * 2, 2), :] = last[14:16]
            if m > 0:
                at = b * 2 * modes + modes + (m - 1) * 4
                ends[pl.ds(at, 2), :] = qkv_v[m, 0:16, cols].astype(jnp.float32)[0:2]
                ends[pl.ds(at + 2, 2), :] = last[14:16]
        return 0

    lax.fori_loop(0, blocks, pack_tail, 0, unroll=4)
    tail_send[...] = tail32[...].astype(jnp.bfloat16)
    pl.semaphore_wait(barrier, n - 1)
    tail_copy = pltpu.make_async_remote_copy(
        src_ref=tail_send,
        dst_ref=tail_recv,
        send_sem=tail_sem.at[0],
        recv_sem=tail_sem.at[1],
        device_id={"seq": lax.rem(me + 1, n)},
        device_id_type=MESH,
    )
    tail_copy.start()

    for load in loads[1:5]:
        load.wait()
    rate = rate_v[...]
    pole = jnp.exp(-rate)
    gain = jnp.sqrt(one_minus_exp(2.0 * rate))
    res = res_v[...]
    prior = prior_v[...]
    for b in range(blocks):
        cut = slice(b * LANES, (b + 1) * LANES)
        put = slice(b * modes, (b + 1) * modes)
        rate_r[put, :] = rate[:, cut]
        table_v[0, put, :] = pole[:, cut]
        gain_r[put, :] = gain[:, cut]
        rg_r[put, :] = (res * gain)[:, cut]
        table_v[1, put, :] = res[:, cut]
        prior_r[put, :] = prior[:, cut]
    stores = [pltpu.make_async_copy(table_v, table_hbm, store_sem.at[0])]
    stores[0].start()

    for m in range(members):
        ext[m, 0:SUBL, :] = jnp.zeros((SUBL, LANES), jnp.float32)

    def taps(m, cols):
        return [cw_v[m, j : j + 1, cols] for j in range(3)]

    def filtered_block(m, cols):
        w0, w1, w2 = taps(m, cols)
        now = qkv_v[m, :, cols].astype(jnp.float32)
        ext[m, SUBL:, :] = now
        return (
            w0 * now
            + w1 * ext[m, SUBL - 1 : SUBL - 1 + tok, :]
            + w2 * ext[m, SUBL - 2 : SUBL - 2 + tok, :]
        )

    def short(b, _):
        cols = pl.ds(pl.multiple_of(b * LANES, LANES), LANES)
        k_feat, v_feat = [filtered_block(m, cols) for m in (1, 2)]
        p_s[pl.ds(pl.multiple_of(b * pitch, SUBL), tok), :] = k_feat * v_feat
        return 0

    lax.fori_loop(0, blocks, short, 0)

    def per_mode(ref):
        return [
            ref[pl.ds(h * SUBL * modes + m, SUBL, stride=modes), :]
            for h in range(halves)
            for m in range(modes)
        ]

    def tokens(ref, t):
        return [ref[pl.ds(h * SUBL * pitch + t, SUBL, stride=pitch), :] for h in range(halves)]

    poles = per_mode(table_v.at[0])

    def horner(t, state):
        now = tokens(p_s, t)
        return tuple(poles[i] * s + now[i // modes] for i, s in enumerate(state))

    zeros = tuple(jnp.zeros((SUBL, LANES), jnp.float32) for _ in range(halves * modes))
    late = lax.fori_loop(2, tok, horner, zeros, unroll=6)

    gains = per_mode(gain_r)
    for i, s in enumerate(late):
        h, m = divmod(i, modes)
        ends[pl.ds(h * SUBL * 2 * modes + m, SUBL, stride=2 * modes), :] = gains[i] * s

    def chunk(index):
        return pl.ds(pl.multiple_of(index * rows, SUBL), rows)

    def wide_chunk(index):
        return pl.ds(pl.multiple_of(index * rows * 2, SUBL), rows * 2)

    sends = []
    for d in range(1, n):
        peer = lax.rem(me + d, n)
        copy = pltpu.make_async_remote_copy(
            src_ref=ends.at[wide_chunk(peer)],
            dst_ref=gath.at[wide_chunk(me)],
            send_sem=s1_sem.at[d],
            recv_sem=r1_sem.at[d],
            device_id={"seq": peer},
            device_id_type=MESH,
        )
        copy.start()
        sends.append(copy)
    gath[wide_chunk(me), :] = ends[wide_chunk(me), :]

    tail_copy.wait_recv()
    tail32[...] = jnp.where(me > 0, tail_recv[...].astype(jnp.float32), 0.0)

    def patch(b, _):
        cols = pl.ds(pl.multiple_of(b * LANES, LANES), LANES)
        feats = []
        for m in (1, 2):
            w0, w1, w2 = taps(m, cols)
            now = qkv_v[m, 0:16, cols].astype(jnp.float32)[0:SUBL]
            ext[m, SUBL - 2 : SUBL, :] = tail32[pl.ds((m * blocks + b) * 2, 2), :]
            ext[m, SUBL : 2 * SUBL, :] = now
            feats.append(
                w0 * now
                + w1 * ext[m, SUBL - 1 : 2 * SUBL - 1, :]
                + w2 * ext[m, SUBL - 2 : 2 * SUBL - 2, :]
            )
        p_s[pl.ds(pl.multiple_of(b * pitch, SUBL), SUBL), :] = feats[0] * feats[1]
        return 0

    lax.fori_loop(0, blocks, patch, 0, unroll=2)
    weights = per_mode(rg_r)

    def scan(t, state):
        now = tokens(p_s, t)
        state = tuple(poles[i] * s + now[i // modes] for i, s in enumerate(state))
        for h in range(halves):
            terms = [weights[i] * state[i] for i in range(h * modes, (h + 1) * modes)]
            while len(terms) > 1:
                terms = [a + b for a, b in zip(terms[::2], terms[1::2])]
            f_s[pl.ds(h * SUBL * pitch + t, SUBL, stride=pitch), :] = terms[0]
        return state

    lax.fori_loop(0, tok, scan, zeros, unroll=4)

    def query(b, _):
        cols = pl.ds(pl.multiple_of(b * LANES, LANES), LANES)
        ext[0, SUBL - 2 : SUBL, :] = tail32[pl.ds(b * 2, 2), :]
        q_s[:, cols] = filtered_block(0, cols)
        return 0

    lax.fori_loop(0, blocks, query, 0)
    stores.append(pltpu.make_async_copy(q_s, q_hbm, store_sem.at[1]))
    stores[1].start()

    for copy in sends:
        copy.wait_recv()
    for copy in sends:
        copy.wait_send()
    states = []
    none = jnp.zeros((1, LANES), jnp.float32)
    for c in range(rows // modes):
        block = me * (rows // modes) + c
        own = pl.ds(pl.multiple_of(block * modes, SUBL), modes)
        cols = pl.ds(pl.multiple_of(block * LANES, LANES), LANES)
        rate_c = rate_r[own, :]
        step = jnp.exp(-rate_c * float(tok))
        late_gain = gain_r[own, :] * jnp.exp(-rate_c * float(tok - 2))
        pole_c = table_v[0, own, :]
        filters = [taps(m, cols) for m in (1, 2)]
        state = prior_r[own, :]
        tails = [(none, none), (none, none)]
        for i in range(n):
            pref[i * rows + c * modes : i * rows + (c + 1) * modes, :] = state
            at = i * rows * 2 + c * modes * 2
            feats = []
            for m in range(2):
                x0, x1, y0, y1 = [
                    gath[at + modes + m * 4 + r : at + modes + m * 4 + r + 1, :]
                    for r in range(4)
                ]
                w0, w1, w2 = filters[m]
                t0, t1 = tails[m]
                feats.append(
                    (w0 * x0 + w1 * t1 + w2 * t0, w0 * x1 + w1 * x0 + w2 * t1)
                )
                tails[m] = (y0, y1)
            early = pole_c * (feats[0][0] * feats[1][0]) + feats[0][1] * feats[1][1]
            state = step * state + (gath[at : at + modes, :] + late_gain * early)
        states.append(state)

    returns = []
    for d in range(1, n):
        peer = lax.rem(me + d, n)
        copy = pltpu.make_async_remote_copy(
            src_ref=pref.at[chunk(peer)],
            dst_ref=inc_hbm.at[chunk(me)],
            send_sem=s2_sem.at[d],
            recv_sem=r2_sem.at[d],
            device_id={"seq": peer},
            device_id_type=MESH,
        )
        copy.start()
        returns.append(copy)
    stores.append(
        pltpu.make_async_copy(pref.at[chunk(me)], inc_hbm.at[chunk(me)], store_sem.at[2])
    )
    stores[2].start()
    for b in range(rows // modes):
        end_v[:, b * LANES : (b + 1) * LANES] = states[b]
    stores.append(pltpu.make_async_copy(end_v, end_hbm, store_sem.at[3]))
    stores[3].start()

    loads[5].wait()
    vocab = emb_v.shape[0]
    which = lax.broadcasted_iota(jnp.int32, (vocab, tok), 0) == ids_ref[...]
    one_hot = jnp.where(which, 1.0, 0.0).astype(jnp.bfloat16)
    wide = 2 * LANES

    def embed(b, _):
        cols = pl.ds(pl.multiple_of(b * wide, wide), wide)
        embedded = lax.dot_general(
            one_hot, emb_v[:, cols], (((0,), (0,)), ((), ())),
            preferred_element_type=jnp.float32,
        )
        for i in range(2):
            part = pl.ds(pl.multiple_of((b * 2 + i) * LANES, LANES), LANES)
            filtered = f_s[pl.ds(pl.multiple_of((b * 2 + i) * pitch, SUBL), tok), :]
            base_v[:, part] = (
                embedded[:, i * LANES : (i + 1) * LANES] + q_s[:, part] * filtered
            )
        return 0

    lax.fori_loop(0, chans // wide, embed, 0)
    stores.append(pltpu.make_async_copy(base_v, base_hbm, store_sem.at[4]))
    stores[4].start()

    tail_copy.wait_send()
    for copy in returns:
        copy.wait_send()
    for store in stores:
        store.wait()
    for copy in returns:
        copy.wait_recv()


def finish_kernel(
    inc_hbm, table_hbm, q_hbm, base_hbm, end_hbm,
    out_hbm, end_out,
    inc, table_v, q_v, base_v, end_v, f_s, out_v,
    load_sem, store_sem,
):
    tok, chans = q_v.shape
    blocks = chans // LANES
    halves = blocks // SUBL
    pitch = tok + SUBL
    modes = SUBL
    half_cols = SUBL * LANES
    loads = [
        pltpu.make_async_copy(src, dst, load_sem.at[i])
        for i, (src, dst) in enumerate(
            (
                (inc_hbm, inc),
                (table_hbm, table_v),
                (end_hbm, end_v),
                (q_hbm, q_v),
                (base_hbm, base_v),
            )
        )
    ]
    for load in loads:
        load.start()
    for load in loads[:2]:
        load.wait()
    inc[...] = table_v[1] * inc[...]
    stores = []
    for h in range(halves):
        spots = [pl.ds(h * SUBL * modes + m, SUBL, stride=modes) for m in range(modes)]
        poles = [table_v.at[0][spot, :] for spot in spots]
        shares = tuple(inc[spot, :] for spot in spots)

        def carried(t, share, h=h, poles=poles):
            share = tuple(p * s for p, s in zip(poles, share))
            terms = list(share)
            while len(terms) > 1:
                terms = [a + b for a, b in zip(terms[::2], terms[1::2])]
            f_s[pl.ds(h * SUBL * pitch + t, SUBL, stride=pitch), :] = terms[0]
            return share

        lax.fori_loop(0, tok, carried, shares, unroll=8)
        if h == 0:
            loads[2].wait()
            stores.append(pltpu.make_async_copy(end_v, end_out, store_sem.at[halves]))
            stores[0].start()
            loads[3].wait()
            loads[4].wait()

        def finish(b, _):
            cols = pl.ds(pl.multiple_of(b * LANES, LANES), LANES)
            filtered = f_s[pl.ds(pl.multiple_of(b * pitch, SUBL), tok), :]
            out_v[:, cols] = (base_v[:, cols] + q_v[:, cols] * filtered).astype(jnp.bfloat16)
            return 0

        lax.fori_loop(h * SUBL, (h + 1) * SUBL, finish, 0)
        span = pl.ds(h * half_cols, half_cols)
        store = pltpu.make_async_copy(out_v.at[:, span], out_hbm.at[:, span], store_sem.at[h])
        store.start()
        stores.append(store)
    for store in stores:
        store.wait()


def fused_body(token_ids, embed_table, hyena_qkv, conv_weights, decay_rates, residues, prior_state):
    n = lax.axis_size("seq")
    members, tok, chans = hyena_qkv.shape
    modes = decay_rates.shape[0]
    blocks = chans // LANES
    f32 = jnp.float32
    rows = blocks * modes
    table = pltpu.VMEM((rows, LANES), f32)
    padded = pltpu.VMEM((blocks * (tok + SUBL), LANES), f32)
    whole = pltpu.VMEM((tok, chans), f32)
    packed = (members * blocks * 2, LANES)
    end_shape = (modes, chans // n)
    scratch = [
        pltpu.VMEM(hyena_qkv.shape, jnp.bfloat16),
        pltpu.VMEM(embed_table.shape, jnp.bfloat16),
        pltpu.VMEM(conv_weights.shape, f32),
        pltpu.VMEM(decay_rates.shape, f32),
        pltpu.VMEM(residues.shape, f32),
        pltpu.VMEM(prior_state.shape, f32),
        pltpu.VMEM(packed, f32),
        pltpu.VMEM(packed, jnp.bfloat16),
        pltpu.VMEM(packed, jnp.bfloat16),
        pltpu.VMEM((members, tok + SUBL, LANES), f32),
        whole,
        padded,
        padded,
        whole,
        pltpu.VMEM(end_shape, f32),
        pltpu.VMEM((2, rows, LANES), f32),
    ] + [table] * 4 + [
        pltpu.VMEM((2 * rows, LANES), f32),
        pltpu.VMEM((2 * rows, LANES), f32),
        table,
    ] + [
        pltpu.SemaphoreType.DMA((6,)),
        pltpu.SemaphoreType.DMA((2,)),
    ] + [pltpu.SemaphoreType.DMA((n,))] * 4 + [pltpu.SemaphoreType.DMA((5,))]
    hbm_spec = pl.BlockSpec(memory_space=pltpu.HBM)
    vmem_spec = pl.BlockSpec(memory_space=pltpu.VMEM)
    room = 60 * 1024 * 1024
    parts = pl.pallas_call(
        functools.partial(fused_kernel, n),
        out_shape=(
            jax.ShapeDtypeStruct((rows, LANES), f32),
            jax.ShapeDtypeStruct((2, rows, LANES), f32),
            jax.ShapeDtypeStruct((tok, chans), f32),
            jax.ShapeDtypeStruct((tok, chans), f32),
            jax.ShapeDtypeStruct(end_shape, f32),
        ),
        in_specs=[vmem_spec] + [hbm_spec] * 6,
        out_specs=(hbm_spec,) * 5,
        scratch_shapes=scratch,
        compiler_params=pltpu.CompilerParams(
            collective_id=0, has_side_effects=True, vmem_limit_bytes=room
        ),
    )(
        token_ids.reshape(1, tok), embed_table, hyena_qkv, conv_weights,
        decay_rates, residues, prior_state,
    )
    return pl.pallas_call(
        finish_kernel,
        out_shape=(
            jax.ShapeDtypeStruct((tok, chans), jnp.bfloat16),
            jax.ShapeDtypeStruct(end_shape, f32),
        ),
        in_specs=[hbm_spec] * 5,
        out_specs=(hbm_spec,) * 2,
        scratch_shapes=[
            table,
            pltpu.VMEM((2, rows, LANES), f32),
            whole,
            whole,
            pltpu.VMEM(end_shape, f32),
            padded,
            pltpu.VMEM((tok, chans), jnp.bfloat16),
            pltpu.SemaphoreType.DMA((5,)),
            pltpu.SemaphoreType.DMA((blocks // SUBL + 1,)),
        ],
        compiler_params=pltpu.CompilerParams(vmem_limit_bytes=room),
    )(*parts)


def body(token_ids, embed_table, hyena_qkv, conv_weights, decay_rates, residues, prior_state):
    n = lax.axis_size("seq")
    members, tok, chans = hyena_qkv.shape
    fits = (
        chans % (n * LANES) == 0
        and chans % (SUBL * LANES) == 0
        and tok % LANES == 0
        and decay_rates.shape[0] == SUBL
        and conv_weights.shape[1] == 3
    )
    run = fused_body if fits else plain_body
    return run(
        token_ids, embed_table, hyena_qkv, conv_weights, decay_rates, residues, prior_state
    )


def solution(mesh):
    return jax.shard_map(
        body,
        mesh=mesh,
        in_specs=(
            P(("groups", "seq")),
            P(None, "tp"),
            P(None, ("groups", "seq"), "tp"),
            P(None, None, "tp"),
            P(None, "tp"),
            P(None, "tp"),
            P("groups", "tp"),
        ),
        out_specs=(P(("groups", "seq"), "tp"), P("groups", ("tp", "seq"))),
        check_vma=False,
    )
```

```python
import functools
import jax
import jax.numpy as jnp
from jax import lax
from jax.experimental import pallas as pl
from jax.experimental.pallas import tpu as pltpu
from jax.sharding import PartitionSpec as P


def shifted(array, axis, by):
    size = lax.axis_size(axis)
    pairs = [(i, i + by) for i in range(size) if 0 <= i + by < size]
    return lax.ppermute(array, axis, pairs)


def short_features(extended, conv_weights, tok_local):
    tap_count = conv_weights.shape[1]
    results = []
    for member in range(3):
        total = jnp.zeros((tok_local, extended.shape[2]), jnp.float32)
        for tap_index in range(tap_count):
            offset = tap_count - 1 - tap_index
            total = total + conv_weights[member, tap_index][None, :] * extended[
                member, offset : offset + tok_local
            ].astype(jnp.float32)
        results.append(total)
    return results


def modal_local(product_in, decay_rates, residues, sub_len):
    tok_local, channels = product_in.shape
    block_count = tok_local // sub_len
    blocks = product_in.reshape(block_count, sub_len, channels)
    spacing = jnp.arange(sub_len, dtype=jnp.float32)
    gain = jnp.sqrt(-jnp.expm1(-2.0 * decay_rates))
    decay_table = jnp.exp(-decay_rates[:, None, :] * spacing[None, :, None])
    kernel = jnp.sum((residues * gain)[:, None, :] * decay_table, axis=0)
    extended = jnp.concatenate(
        [kernel[::-1], jnp.zeros((sub_len - 1, channels), jnp.float32)], axis=0
    )
    toeplitz = jnp.stack(
        [extended[sub_len - 1 - row : 2 * sub_len - 1 - row] for row in range(sub_len)], axis=0
    )
    inner = jnp.einsum("tsc,bsc->btc", toeplitz, blocks, precision=lax.Precision.HIGHEST)
    tail_weight = gain[:, None, :] * jnp.exp(
        -decay_rates[:, None, :] * (sub_len - 1 - spacing)[None, :, None]
    )
    closing = jnp.einsum("bsc,msc->bmc", blocks, tail_weight, precision=lax.Precision.HIGHEST)
    per_block = jnp.exp(-decay_rates * sub_len)

    def advance(carry, piece):
        return (per_block * carry + piece, carry)

    local_end, starts = lax.scan(advance, jnp.zeros_like(decay_rates), closing)
    return (inner, starts, local_end)


def modal_readout(inner, starts, incoming, decay_rates, residues, sub_len):
    block_count = starts.shape[0]
    block_pos = jnp.arange(block_count, dtype=jnp.float32) * sub_len
    opening = (
        starts + jnp.exp(-decay_rates[None, :, :] * block_pos[:, None, None]) * incoming[None, :, :]
    )
    spacing = jnp.arange(sub_len, dtype=jnp.float32)
    readout = residues[:, None, :] * jnp.exp(
        -decay_rates[:, None, :] * (spacing + 1.0)[None, :, None]
    )
    outer = jnp.einsum("bmc,mtc->btc", opening, readout, precision=lax.Precision.HIGHEST)
    return (inner + outer).reshape(block_count * sub_len, inner.shape[2])


def plain_body(token_ids, embed_table, hyena_qkv, conv_weights, decay_rates, residues, prior_state):
    tok_local = hyena_qkv.shape[1]
    tap_count = conv_weights.shape[1]
    seq_count = lax.axis_size("seq")
    seq_index = lax.axis_index("seq")
    tails_local = hyena_qkv[:, tok_local - (tap_count - 1) :, :]
    tails_prev = shifted(tails_local, "seq", 1)
    extended = jnp.concatenate([tails_prev, hyena_qkv], axis=1)
    q_feat, k_feat, v_feat = short_features(extended, conv_weights, tok_local)
    product_in = k_feat * v_feat
    sub_len = 16
    inner, starts, local_end = modal_local(product_in, decay_rates, residues, sub_len)
    piece = lax.all_gather(local_end[None], "seq", axis=0, tiled=True)
    count = piece.shape[0]
    sources = jnp.arange(count, dtype=jnp.int32)
    gap_len = jnp.maximum(seq_index - 1 - sources, 0).astype(jnp.float32) * tok_local
    factors = jnp.where(
        (sources < seq_index)[:, None, None],
        jnp.exp(-decay_rates[None, :, :] * gap_len[:, None, None]),
        0.0,
    )
    folded = jnp.sum(factors * piece, axis=0)
    incoming = (
        folded + jnp.exp(-decay_rates * (seq_index.astype(jnp.float32) * tok_local)) * prior_state
    )
    filtered = modal_readout(inner, starts, incoming, decay_rates, residues, sub_len)
    vocab_ids = jnp.arange(embed_table.shape[0], dtype=jnp.int32)
    one_hot = (token_ids[:, None] == vocab_ids[None, :]).astype(jnp.bfloat16)
    embedded = jnp.dot(one_hot, embed_table, preferred_element_type=jnp.float32)
    hyena_out = (embedded + q_feat * filtered).astype(jnp.bfloat16)
    lag_after = (seq_count - 1 - seq_index).astype(jnp.float32) * tok_local
    end_term = jnp.exp(-decay_rates * lag_after) * local_end
    end_share = lax.psum_scatter(end_term, "seq", scatter_dimension=1, tiled=True)
    share_cols = end_share.shape[1]
    rate_share = lax.dynamic_slice_in_dim(decay_rates, seq_index * share_cols, share_cols, 1)
    prior_share = lax.dynamic_slice_in_dim(prior_state, seq_index * share_cols, share_cols, 1)
    end_state = end_share + jnp.exp(-rate_share * float(seq_count * tok_local)) * prior_share
    return (hyena_out, end_state)


LANES = 128
SUBL = 8
MESH = pl.DeviceIdType.MESH


def one_minus_exp(y):
    series = jnp.ones_like(y)
    for k in range(9, 1, -1):
        series = 1.0 - (y / k) * series
    return jnp.where(y < 0.5, y * series, 1.0 - jnp.exp(-y))


def fused_kernel(
    n, ids_ref, emb_hbm, qkv_hbm, cw_hbm, rate_hbm, res_hbm, prior_hbm,
    inc_hbm, table_hbm, q_hbm, base_hbm, end_hbm,
    qkv_v, emb_v, cw_v, rate_v, res_v, prior_v,
    tail32, tail_send, tail_recv, ext, q_s, p_s, f_s, base_v, end_v, table_v,
    rate_r, gain_r, rg_r, prior_r, ends, gath, pref,
    load_sem, tail_sem, s1_sem, r1_sem, s2_sem, r2_sem, store_sem,
):
    members, tok, chans = qkv_v.shape
    blocks = chans // LANES
    halves = blocks // SUBL
    pitch = tok + SUBL
    modes = SUBL
    rows = blocks // n * modes
    me = lax.axis_index("seq")

    barrier = pltpu.get_barrier_semaphore()
    for d in range(1, n):
        pl.semaphore_signal(
            barrier, inc=1, device_id={"seq": lax.rem(me + d, n)}, device_id_type=MESH
        )

    loads = [
        pltpu.make_async_copy(src, dst, load_sem.at[i])
        for i, (src, dst) in enumerate(
            (
                (qkv_hbm, qkv_v),
                (rate_hbm, rate_v),
                (res_hbm, res_v),
                (prior_hbm, prior_v),
                (cw_hbm, cw_v),
                (emb_hbm, emb_v),
            )
        )
    ]
    for load in loads:
        load.start()

    loads[0].wait()

    def pack_tail(b, _):
        cols = pl.ds(pl.multiple_of(b * LANES, LANES), LANES)
        for m in range(members):
            last = qkv_v[m, tok - 16 : tok, cols].astype(jnp.float32)
            tail32[pl.ds((m * blocks + b) * 2, 2), :] = last[14:16]
            if m > 0:
                at = b * 2 * modes + modes + (m - 1) * 4
                ends[pl.ds(at, 2), :] = qkv_v[m, 0:16, cols].astype(jnp.float32)[0:2]
                ends[pl.ds(at + 2, 2), :] = last[14:16]
        return 0

    lax.fori_loop(0, blocks, pack_tail, 0, unroll=8)
    tail_send[...] = tail32[...].astype(jnp.bfloat16)
    pl.semaphore_wait(barrier, n - 1)
    tail_copy = pltpu.make_async_remote_copy(
        src_ref=tail_send,
        dst_ref=tail_recv,
        send_sem=tail_sem.at[0],
        recv_sem=tail_sem.at[1],
        device_id={"seq": lax.rem(me + 1, n)},
        device_id_type=MESH,
    )
    tail_copy.start()

    for load in loads[1:5]:
        load.wait()
    rate = rate_v[...]
    pole = jnp.exp(-rate)
    gain = jnp.sqrt(one_minus_exp(2.0 * rate))
    res = res_v[...]
    prior = prior_v[...]
    for b in range(blocks):
        cut = slice(b * LANES, (b + 1) * LANES)
        put = slice(b * modes, (b + 1) * modes)
        rate_r[put, :] = rate[:, cut]
        table_v[0, put, :] = pole[:, cut]
        gain_r[put, :] = gain[:, cut]
        rg_r[put, :] = (res * gain)[:, cut]
        table_v[1, put, :] = res[:, cut]
        prior_r[put, :] = prior[:, cut]
    stores = [pltpu.make_async_copy(table_v, table_hbm, store_sem.at[0])]
    stores[0].start()

    for m in range(members):
        ext[m, 0:SUBL, :] = jnp.zeros((SUBL, LANES), jnp.float32)

    def taps(m, cols):
        return [cw_v[m, j : j + 1, cols] for j in range(3)]

    def filtered_block(m, cols):
        w0, w1, w2 = taps(m, cols)
        now = qkv_v[m, :, cols].astype(jnp.float32)
        ext[m, SUBL:, :] = now
        return (
            w0 * now
            + w1 * ext[m, SUBL - 1 : SUBL - 1 + tok, :]
            + w2 * ext[m, SUBL - 2 : SUBL - 2 + tok, :]
        )

    def short(b, _):
        cols = pl.ds(pl.multiple_of(b * LANES, LANES), LANES)
        k_feat, v_feat = [filtered_block(m, cols) for m in (1, 2)]
        p_s[pl.ds(pl.multiple_of(b * pitch, SUBL), tok), :] = k_feat * v_feat
        return 0

    lax.fori_loop(0, blocks, short, 0, unroll=2)

    def per_mode(ref):
        return [
            ref[pl.ds(h * SUBL * modes + m, SUBL, stride=modes), :]
            for h in range(halves)
            for m in range(modes)
        ]

    def tokens(ref, t):
        return [ref[pl.ds(h * SUBL * pitch + t, SUBL, stride=pitch), :] for h in range(halves)]

    poles = per_mode(table_v.at[0])

    def horner(t, state):
        now = tokens(p_s, t)
        return tuple(poles[i] * s + now[i // modes] for i, s in enumerate(state))

    zeros = tuple(jnp.zeros((SUBL, LANES), jnp.float32) for _ in range(halves * modes))
    late = lax.fori_loop(2, tok, horner, zeros, unroll=14)

    gains = per_mode(gain_r)
    for i, s in enumerate(late):
        h, m = divmod(i, modes)
        ends[pl.ds(h * SUBL * 2 * modes + m, SUBL, stride=2 * modes), :] = gains[i] * s

    def chunk(index):
        return pl.ds(pl.multiple_of(index * rows, SUBL), rows)

    def wide_chunk(index):
        return pl.ds(pl.multiple_of(index * rows * 2, SUBL), rows * 2)

    sends = []
    for d in range(1, n):
        peer = lax.rem(me + d, n)
        copy = pltpu.make_async_remote_copy(
            src_ref=ends.at[wide_chunk(peer)],
            dst_ref=gath.at[wide_chunk(me)],
            send_sem=s1_sem.at[d],
            recv_sem=r1_sem.at[d],
            device_id={"seq": peer},
            device_id_type=MESH,
        )
        copy.start()
        sends.append(copy)
    gath[wide_chunk(me), :] = ends[wide_chunk(me), :]

    tail_copy.wait_recv()
    tail32[...] = jnp.where(me > 0, tail_recv[...].astype(jnp.float32), 0.0)

    def patch(b, _):
        cols = pl.ds(pl.multiple_of(b * LANES, LANES), LANES)
        feats = []
        for m in (1, 2):
            w0, w1, w2 = taps(m, cols)
            now = qkv_v[m, 0:16, cols].astype(jnp.float32)[0:SUBL]
            ext[m, SUBL - 2 : SUBL, :] = tail32[pl.ds((m * blocks + b) * 2, 2), :]
            ext[m, SUBL : 2 * SUBL, :] = now
            feats.append(
                w0 * now
                + w1 * ext[m, SUBL - 1 : 2 * SUBL - 1, :]
                + w2 * ext[m, SUBL - 2 : 2 * SUBL - 2, :]
            )
        p_s[pl.ds(pl.multiple_of(b * pitch, SUBL), SUBL), :] = feats[0] * feats[1]
        return 0

    lax.fori_loop(0, blocks, patch, 0, unroll=2)
    weights = per_mode(rg_r)

    def scan(t, state):
        now = tokens(p_s, t)
        state = tuple(poles[i] * s + now[i // modes] for i, s in enumerate(state))
        for h in range(halves):
            terms = [weights[i] * state[i] for i in range(h * modes, (h + 1) * modes)]
            while len(terms) > 1:
                terms = [a + b for a, b in zip(terms[::2], terms[1::2])]
            f_s[pl.ds(h * SUBL * pitch + t, SUBL, stride=pitch), :] = terms[0]
        return state

    lax.fori_loop(0, tok, scan, zeros, unroll=4)

    def query(b, _):
        cols = pl.ds(pl.multiple_of(b * LANES, LANES), LANES)
        ext[0, SUBL - 2 : SUBL, :] = tail32[pl.ds(b * 2, 2), :]
        q_s[:, cols] = filtered_block(0, cols)
        return 0

    lax.fori_loop(0, blocks, query, 0)
    stores.append(pltpu.make_async_copy(q_s, q_hbm, store_sem.at[1]))
    stores[1].start()

    for copy in sends:
        copy.wait_recv()
    for copy in sends:
        copy.wait_send()
    states = []
    none = jnp.zeros((1, LANES), jnp.float32)
    for c in range(rows // modes):
        block = me * (rows // modes) + c
        own = pl.ds(pl.multiple_of(block * modes, SUBL), modes)
        cols = pl.ds(pl.multiple_of(block * LANES, LANES), LANES)
        rate_c = rate_r[own, :]
        step = jnp.exp(-rate_c * float(tok))
        late_gain = gain_r[own, :] * jnp.exp(-rate_c * float(tok - 2))
        pole_c = table_v[0, own, :]
        filters = [taps(m, cols) for m in (1, 2)]
        state = prior_r[own, :]
        tails = [(none, none), (none, none)]
        for i in range(n):
            pref[i * rows + c * modes : i * rows + (c + 1) * modes, :] = state
            at = i * rows * 2 + c * modes * 2
            feats = []
            for m in range(2):
                x0, x1, y0, y1 = [
                    gath[at + modes + m * 4 + r : at + modes + m * 4 + r + 1, :]
                    for r in range(4)
                ]
                w0, w1, w2 = filters[m]
                t0, t1 = tails[m]
                feats.append(
                    (w0 * x0 + w1 * t1 + w2 * t0, w0 * x1 + w1 * x0 + w2 * t1)
                )
                tails[m] = (y0, y1)
            early = pole_c * (feats[0][0] * feats[1][0]) + feats[0][1] * feats[1][1]
            state = step * state + (gath[at : at + modes, :] + late_gain * early)
        states.append(state)

    returns = []
    for d in range(1, n):
        peer = lax.rem(me + d, n)
        copy = pltpu.make_async_remote_copy(
            src_ref=pref.at[chunk(peer)],
            dst_ref=inc_hbm.at[chunk(me)],
            send_sem=s2_sem.at[d],
            recv_sem=r2_sem.at[d],
            device_id={"seq": peer},
            device_id_type=MESH,
        )
        copy.start()
        returns.append(copy)
    stores.append(
        pltpu.make_async_copy(pref.at[chunk(me)], inc_hbm.at[chunk(me)], store_sem.at[2])
    )
    stores[2].start()
    for b in range(rows // modes):
        end_v[:, b * LANES : (b + 1) * LANES] = states[b]
    stores.append(pltpu.make_async_copy(end_v, end_hbm, store_sem.at[3]))
    stores[3].start()

    loads[5].wait()
    vocab = emb_v.shape[0]
    which = lax.broadcasted_iota(jnp.int32, (vocab, tok), 0) == ids_ref[...]
    one_hot = jnp.where(which, 1.0, 0.0).astype(jnp.bfloat16)
    wide = 2 * LANES

    def embed(b, _):
        cols = pl.ds(pl.multiple_of(b * wide, wide), wide)
        embedded = lax.dot_general(
            one_hot, emb_v[:, cols], (((0,), (0,)), ((), ())),
            preferred_element_type=jnp.float32,
        )
        for i in range(2):
            part = pl.ds(pl.multiple_of((b * 2 + i) * LANES, LANES), LANES)
            filtered = f_s[pl.ds(pl.multiple_of((b * 2 + i) * pitch, SUBL), tok), :]
            base_v[:, part] = (
                embedded[:, i * LANES : (i + 1) * LANES] + q_s[:, part] * filtered
            )
        return 0

    lax.fori_loop(0, chans // wide, embed, 0)
    stores.append(pltpu.make_async_copy(base_v, base_hbm, store_sem.at[4]))
    stores[4].start()

    tail_copy.wait_send()
    for copy in returns:
        copy.wait_send()
    for store in stores:
        store.wait()
    for copy in returns:
        copy.wait_recv()


def finish_kernel(
    inc_hbm, table_hbm, q_hbm, base_hbm, end_hbm,
    out_hbm, end_out,
    inc, table_v, q_v, base_v, end_v, f_s, out_v,
    load_sem, store_sem,
):
    tok, chans = q_v.shape
    blocks = chans // LANES
    halves = blocks // SUBL
    pitch = tok + SUBL
    modes = SUBL
    half_cols = SUBL * LANES
    loads = [
        pltpu.make_async_copy(src, dst, load_sem.at[i])
        for i, (src, dst) in enumerate(
            (
                (inc_hbm, inc),
                (table_hbm, table_v),
                (end_hbm, end_v),
                (q_hbm, q_v),
                (base_hbm, base_v),
            )
        )
    ]
    for load in loads:
        load.start()
    for load in loads[:2]:
        load.wait()
    inc[...] = table_v[1] * inc[...]
    stores = []
    for h in range(halves):
        spots = [pl.ds(h * SUBL * modes + m, SUBL, stride=modes) for m in range(modes)]
        poles = [table_v.at[0][spot, :] for spot in spots]
        shares = tuple(inc[spot, :] for spot in spots)

        def carried(t, share, h=h, poles=poles):
            share = tuple(p * s for p, s in zip(poles, share))
            terms = list(share)
            while len(terms) > 1:
                terms = [a + b for a, b in zip(terms[::2], terms[1::2])]
            f_s[pl.ds(h * SUBL * pitch + t, SUBL, stride=pitch), :] = terms[0]
            return share

        lax.fori_loop(0, tok, carried, shares, unroll=8)
        if h == 0:
            loads[2].wait()
            stores.append(pltpu.make_async_copy(end_v, end_out, store_sem.at[2 * halves]))
            stores[0].start()
            loads[3].wait()
            loads[4].wait()

        def finish(b, _):
            cols = pl.ds(pl.multiple_of(b * LANES, LANES), LANES)
            filtered = f_s[pl.ds(pl.multiple_of(b * pitch, SUBL), tok), :]
            out_v[:, cols] = (base_v[:, cols] + q_v[:, cols] * filtered).astype(jnp.bfloat16)
            return 0

        for part in range(2 * h, 2 * h + 2):
            lax.fori_loop(part * SUBL // 2, (part + 1) * SUBL // 2, finish, 0, unroll=2)
            span = pl.ds(part * half_cols // 2, half_cols // 2)
            store = pltpu.make_async_copy(
                out_v.at[:, span], out_hbm.at[:, span], store_sem.at[part]
            )
            store.start()
            stores.append(store)
    for store in stores:
        store.wait()


def fused_body(token_ids, embed_table, hyena_qkv, conv_weights, decay_rates, residues, prior_state):
    n = lax.axis_size("seq")
    members, tok, chans = hyena_qkv.shape
    modes = decay_rates.shape[0]
    blocks = chans // LANES
    f32 = jnp.float32
    rows = blocks * modes
    table = pltpu.VMEM((rows, LANES), f32)
    padded = pltpu.VMEM((blocks * (tok + SUBL), LANES), f32)
    whole = pltpu.VMEM((tok, chans), f32)
    packed = (members * blocks * 2, LANES)
    end_shape = (modes, chans // n)
    scratch = [
        pltpu.VMEM(hyena_qkv.shape, jnp.bfloat16),
        pltpu.VMEM(embed_table.shape, jnp.bfloat16),
        pltpu.VMEM(conv_weights.shape, f32),
        pltpu.VMEM(decay_rates.shape, f32),
        pltpu.VMEM(residues.shape, f32),
        pltpu.VMEM(prior_state.shape, f32),
        pltpu.VMEM(packed, f32),
        pltpu.VMEM(packed, jnp.bfloat16),
        pltpu.VMEM(packed, jnp.bfloat16),
        pltpu.VMEM((members, tok + SUBL, LANES), f32),
        whole,
        padded,
        padded,
        whole,
        pltpu.VMEM(end_shape, f32),
        pltpu.VMEM((2, rows, LANES), f32),
    ] + [table] * 4 + [
        pltpu.VMEM((2 * rows, LANES), f32),
        pltpu.VMEM((2 * rows, LANES), f32),
        table,
    ] + [
        pltpu.SemaphoreType.DMA((6,)),
        pltpu.SemaphoreType.DMA((2,)),
    ] + [pltpu.SemaphoreType.DMA((n,))] * 4 + [pltpu.SemaphoreType.DMA((5,))]
    hbm_spec = pl.BlockSpec(memory_space=pltpu.HBM)
    vmem_spec = pl.BlockSpec(memory_space=pltpu.VMEM)
    room = 60 * 1024 * 1024
    parts = pl.pallas_call(
        functools.partial(fused_kernel, n),
        out_shape=(
            jax.ShapeDtypeStruct((rows, LANES), f32),
            jax.ShapeDtypeStruct((2, rows, LANES), f32),
            jax.ShapeDtypeStruct((tok, chans), f32),
            jax.ShapeDtypeStruct((tok, chans), f32),
            jax.ShapeDtypeStruct(end_shape, f32),
        ),
        in_specs=[vmem_spec] + [hbm_spec] * 6,
        out_specs=(hbm_spec,) * 5,
        scratch_shapes=scratch,
        compiler_params=pltpu.CompilerParams(
            collective_id=0, has_side_effects=True, vmem_limit_bytes=room
        ),
    )(
        token_ids.reshape(1, tok), embed_table, hyena_qkv, conv_weights,
        decay_rates, residues, prior_state,
    )
    return pl.pallas_call(
        finish_kernel,
        out_shape=(
            jax.ShapeDtypeStruct((tok, chans), jnp.bfloat16),
            jax.ShapeDtypeStruct(end_shape, f32),
        ),
        in_specs=[hbm_spec] * 5,
        out_specs=(hbm_spec,) * 2,
        scratch_shapes=[
            table,
            pltpu.VMEM((2, rows, LANES), f32),
            whole,
            whole,
            pltpu.VMEM(end_shape, f32),
            padded,
            pltpu.VMEM((tok, chans), jnp.bfloat16),
            pltpu.SemaphoreType.DMA((5,)),
            pltpu.SemaphoreType.DMA((2 * (blocks // SUBL) + 1,)),
        ],
        compiler_params=pltpu.CompilerParams(vmem_limit_bytes=room),
    )(*parts)


def body(token_ids, embed_table, hyena_qkv, conv_weights, decay_rates, residues, prior_state):
    n = lax.axis_size("seq")
    members, tok, chans = hyena_qkv.shape
    fits = (
        chans % (n * LANES) == 0
        and chans % (SUBL * LANES) == 0
        and tok % LANES == 0
        and decay_rates.shape[0] == SUBL
        and conv_weights.shape[1] == 3
    )
    run = fused_body if fits else plain_body
    return run(
        token_ids, embed_table, hyena_qkv, conv_weights, decay_rates, residues, prior_state
    )


def solution(mesh):
    return jax.shard_map(
        body,
        mesh=mesh,
        in_specs=(
            P(("groups", "seq")),
            P(None, "tp"),
            P(None, ("groups", "seq"), "tp"),
            P(None, None, "tp"),
            P(None, "tp"),
            P(None, "tp"),
            P("groups", "tp"),
        ),
        out_specs=(P(("groups", "seq"), "tp"), P("groups", ("tp", "seq"))),
        check_vma=False,
    )
```
